128 devices in a mesh: dp: 8 (over x, y_hi), seq: 16 (over y_lo, z, core).
Axes of the slice: x: 4, y: 4 (y_hi: 2, y_lo: 2; y = y_hi * 2 + y_lo), z: 4, core: 2. Of those that a mesh axis runs over, the one named last changes fastest.
Arguments:
- queries: bfloat16 [8, 3072, 1536], P('dp', 'seq'), may hold values from -12 to 12
- keys_in: bfloat16 [8, 3072, 1536], P('dp', 'seq'), may hold values from -6 to 6
- values_in: bfloat16 [8, 3072, 1536], P('dp', 'seq'), may hold values from -6 to 6
- lengths: int32 [8], P('dp'), may hold values from 768 to 3072, as said below
- kernel: float32 [31, 1536], replicated, may hold values from -1.5 to 1.5
- cotangent: bfloat16 [8, 3072, 1536], P('dp', 'seq'), may hold values from -6 to 6
Outputs:
- block_out: bfloat16 [8, 3072, 1536], P('dp', 'seq')
- query_grad: bfloat16 [8, 3072, 1536], P('dp', 'seq')
- key_grad: bfloat16 [8, 3072, 1536], P('dp', 'seq')
- value_grad: bfloat16 [8, 3072, 1536], P('dp', 'seq')
- kernel_grad: float32 [31, 1536], replicated
The draws below stay inside these ranges and needn't reach their ends.
Inputs may be any that keep to these rules, and one draw needn't show every extreme that they name: `lengths`: frames at or past an utterance's length are padding.
All inputs are finite; a program needn't handle non-finite values.
Results may differ from the reference program's by a relative error of at most 0.025.
Values may be sent and summed in bfloat16 or wider, within the bound.
No kernel may reach another device: no remote copies, remote signals or barrier semaphores. Data moves between devices by JAX's collectives and lax.ppermute only.
A program may use at most 64 MiB of HBM per device.

```python
import jax
import jax.numpy as jnp
from jax import lax

HEADS = 16
HEAD_DIM = 96
KERNEL = 31
WIDTH = 1536
FRAMES = 3072
UTTS = 8


def draw_queries(key, part):
    key = jax.random.fold_in(key, 1)
    drawn = jnp.clip(2.0 * jax.random.normal(key, (UTTS, FRAMES, WIDTH), jnp.float32), -12.0, 12.0)
    return drawn.astype(jnp.bfloat16)


def draw_keys_in(key, part):
    key = jax.random.fold_in(key, 2)
    drawn = jnp.clip(jax.random.normal(key, (UTTS, FRAMES, WIDTH), jnp.float32), -6.0, 6.0)
    return drawn.astype(jnp.bfloat16)


def draw_lengths(key, part):
    key = jax.random.fold_in(key, 3)
    first_key, second_key = jax.random.split(key)
    drawn = jax.random.randint(first_key, (UTTS,), FRAMES // 4, FRAMES + 1)
    longest = jax.random.randint(second_key, (), 0, UTTS)
    places = jnp.arange(UTTS)
    drawn = jnp.where(places == longest, FRAMES, drawn)
    drawn = jnp.where(places == (longest + 1) % UTTS, FRAMES // 4, drawn)
    return drawn.astype(jnp.int32)


def steps_of(key, shape, pieces, smallest, top_value):
    def one(axis_at, shards_of):
        steps = jax.random.uniform(jax.random.fold_in(jax.random.fold_in(key, 6), axis_at), (shards_of,), jnp.float32, smallest / len(pieces), top_value / len(pieces))
        return jnp.repeat(jnp.exp(steps), shape[axis_at] // shards_of).reshape((-1,) + (1,) * (len(shape) - axis_at - 1))

    factor_of = one(*pieces[0])
    for cut in pieces[1:]:
        factor_of = factor_of * one(*cut)
    return factor_of


def scatter_about(key, shape, spread, most, pieces=(), held_as=jnp.bfloat16):
    entries = jax.random.normal(key, shape, jnp.float32) * spread
    if len(pieces) > 0:
        entries = steps_of(key, shape, pieces, -0.22, 0.18) * entries
    return jnp.clip(entries, min=-most, max=most).astype(held_as)


def setup_inputs(seed: int = 0) -> dict:
    arg_keys = jax.random.split(jax.random.key(seed), 7)
    queries = draw_queries(jax.random.fold_in(arg_keys[6], 71), 0)
    keys_in = draw_keys_in(jax.random.fold_in(arg_keys[6], 71), 0)
    values_in = scatter_about(arg_keys[2], (UTTS, FRAMES, WIDTH), 1.0, 6.0, ((0, 8), (1, 16)))
    lengths = draw_lengths(jax.random.fold_in(arg_keys[6], 71), 0)
    kernel = scatter_about(arg_keys[4], (KERNEL, WIDTH), 0.25, 1.5, (), jnp.float32)
    cotangent = scatter_about(arg_keys[5], (UTTS, FRAMES, WIDTH), 1.0, 6.0, ((0, 8), (1, 16)))
    return dict(queries=queries, keys_in=keys_in, values_in=values_in, lengths=lengths, kernel=kernel, cotangent=cotangent)


masked_score = -1e+30

def attend(query_f, keys_f, values_f, key_ok):
    count = query_f.shape[0]
    block_rows = min(512, count)
    scaling = query_f.shape[2] ** (-0.5)

    def one_block(query_block):
        scores = jnp.einsum('qhd,khd->hqk', query_block, keys_f, precision=lax.Precision.HIGHEST) * scaling
        scores = jnp.where(key_ok[None, None, :], scores, masked_score)
        top_score = lax.optimization_barrier(jnp.max(scores, axis=-1, keepdims=True))
        expo = jnp.exp(scores - top_score)
        probs = lax.optimization_barrier((expo / lax.optimization_barrier(jnp.sum(expo, axis=-1, keepdims=True))).astype(jnp.bfloat16))
        probs = probs.astype(jnp.float32)
        return jnp.einsum('hqk,khd->qhd', probs, values_f, precision=lax.Precision.HIGHEST)
    stacked = query_f.reshape(count // block_rows, block_rows, query_f.shape[1], query_f.shape[2])
    result = lax.map(jax.checkpoint(one_block), stacked)
    return result.reshape(query_f.shape)

def depth_apply(padded, kernel, count):
    summed = jnp.zeros((count, kernel.shape[1]), jnp.float32)
    for offset in range(kernel.shape[0]):
        summed = summed + kernel[offset][None, :] * padded[offset:offset + count]
    return summed

def reference(queries, keys_in, values_in, lengths, kernel, cotangent):
    half = (KERNEL - 1) // 2
    outputs, qgrads, kgrads, vgrads = ([], [], [], [])
    kernel_grad = jnp.zeros((KERNEL, WIDTH), jnp.float32)
    for utter in range(UTTS):
        key_ok = jnp.arange(FRAMES) < lengths[utter]
        frame_mask = key_ok.astype(jnp.float32)[:, None]
        shape3 = (FRAMES, HEADS, HEAD_DIM)
        query_f = queries[utter].astype(jnp.float32).reshape(shape3)
        keys_f = keys_in[utter].astype(jnp.float32).reshape(shape3)
        values_f = values_in[utter].astype(jnp.float32).reshape(shape3)
        attended, pullback = jax.vjp(lambda first_arg, second_arg, third_arg: attend(first_arg, second_arg, third_arg, key_ok), query_f, keys_f, values_f)
        context = (attended.reshape(FRAMES, WIDTH) * frame_mask).astype(jnp.bfloat16)
        context_f = context.astype(jnp.float32)
        padded = jnp.pad(context_f, ((half, half), (0, 0)))
        outputs.append(((context_f + depth_apply(padded, kernel, FRAMES)) * frame_mask).astype(jnp.bfloat16))
        masked_grad = cotangent[utter].astype(jnp.float32) * frame_mask
        grad_padded = jnp.pad(masked_grad, ((half, half), (0, 0)))
        taps = jnp.stack([lax.optimization_barrier(jnp.sum(masked_grad * padded[offset:offset + FRAMES], axis=0)) for offset in range(KERNEL)])
        kernel_grad = kernel_grad + taps
        context_grad = ((masked_grad + depth_apply(grad_padded, kernel[::-1], FRAMES)) * frame_mask).astype(jnp.bfloat16)
        dquery, dkeys, dvalues = pullback(context_grad.astype(jnp.float32).reshape(shape3))
        qgrads.append(dquery.reshape(FRAMES, WIDTH).astype(jnp.bfloat16))
        kgrads.append(dkeys.reshape(FRAMES, WIDTH).astype(jnp.bfloat16))
        vgrads.append(dvalues.reshape(FRAMES, WIDTH).astype(jnp.bfloat16))
    return (jnp.stack(outputs), jnp.stack(qgrads), jnp.stack(kgrads), jnp.stack(vgrads), kernel_grad)
```

```python
import functools

import jax
import jax.numpy as jnp
from jax import lax
from jax.experimental import pallas as pl
from jax.experimental.pallas import tpu as pltpu
from jax.sharding import PartitionSpec as P

HEAD_DIM = 96
LANES = 128
TAPS = 31
HALF = 15
FRONT = 32
QUERY_BLOCK = 512
KEY_CHUNK = 384
MASKED = -1e30
LOG2E = 1.4426950408889634

NT = (((1,), (1,)), ((), ()))
NN = (((1,), (0,)), ((), ()))
F32 = jnp.float32
BF16 = jnp.bfloat16


def dot(a, b, dims=NN):
    return lax.dot_general(a, b, dims, preferred_element_type=F32)


def lanes_like(x):
    return lax.broadcasted_iota(jnp.int32, x.shape, 1)


def spread(t0, t1, t2):
    lane = lanes_like(t0)
    first = t0
    second = jnp.where(lane < 32, pltpu.roll(t0, 32, 1), pltpu.roll(t1, 32, 1))
    third = jnp.where(lane < 64, pltpu.roll(t1, 64, 1), pltpu.roll(t2, 64, 1))
    fourth = pltpu.roll(t2, 96, 1)
    return first, second, third, fourth


def squeeze(a, b, c, d):
    lane = lanes_like(a)
    b, c = pltpu.roll(b, 96, 1), pltpu.roll(c, 64, 1)
    return (
        jnp.where(lane < 96, a, b),
        jnp.where(lane < 64, b, c),
        jnp.where(lane < 32, c, pltpu.roll(d, 32, 1)),
    )


def tiles_of(ref, at):
    return [ref[at + (slice(None), slice(LANES * i, LANES * (i + 1)))].astype(F32) for i in range(3)]


def pack_kernel(a_ref, b_ref, c_ref, d_ref, out_ref):
    heads = [spread(*tiles_of(ref, ())) for ref in (a_ref, b_ref, c_ref, d_ref)]
    for h in range(4):
        for i, tile in enumerate(squeeze(*[of[h] for of in heads])):
            out_ref[h, :, LANES * i : LANES * (i + 1)] = tile.astype(BF16)


def unpack_kernel(in_ref, a_ref, b_ref, c_ref, d_ref):
    heads = [spread(*tiles_of(in_ref, (h,))) for h in range(4)]
    for j, ref in enumerate((a_ref, b_ref, c_ref, d_ref)):
        for i, tile in enumerate(squeeze(*[of[j] for of in heads])):
            ref[:, LANES * i : LANES * (i + 1)] = tile.astype(BF16)


def pack(arrays):
    frames, width = arrays[0].shape
    group = 4 * HEAD_DIM
    return pl.pallas_call(
        pack_kernel,
        grid=(width // group,),
        in_specs=[pl.BlockSpec((frames, group), lambda g: (0, g))] * 4,
        out_specs=pl.BlockSpec((4, frames, group), lambda g: (g, 0, 0)),
        out_shape=jax.ShapeDtypeStruct((width // HEAD_DIM, frames, group), BF16),
        name="pack",
    )(*arrays)


def unpack(packed):
    heads, frames, group = packed.shape
    return pl.pallas_call(
        unpack_kernel,
        grid=(heads // 4,),
        in_specs=[pl.BlockSpec((4, frames, group), lambda g: (g, 0, 0))],
        out_specs=[pl.BlockSpec((frames, group), lambda g: (0, g))] * 4,
        out_shape=[jax.ShapeDtypeStruct((frames, heads * HEAD_DIM), BF16)] * 4,
        name="unpack",
    )(packed)


def core_kernel(
    len_ref, x_ref, taps_ref, out_ref, grad_ref,
    qx, kx, vx, kt, vt, s_buf, e_buf, cot, ctx, cgr, bo, dq, dk, dv, ot, dqt, acc,
):
    blocks, rows, _ = x_ref.shape
    frames = blocks * rows
    length = len_ref[0]
    scaling = HEAD_DIM ** (-0.5)
    c = scaling * LOG2E
    chunks = frames // KEY_CHUNK
    step = QUERY_BLOCK // chunks

    for ref in (cot, ctx):
        ref[0:FRONT, :] = jnp.zeros((FRONT, LANES), F32)
        ref[FRONT + frames :, :] = jnp.zeros((ref.shape[0] - FRONT - frames, LANES), F32)
    dk[...] = jnp.zeros_like(dk)
    dv[...] = jnp.zeros_like(dv)
    acc[...] = jnp.zeros_like(acc)

    def load(n, _):
        t0 = pl.multiple_of(n * rows, rows)
        q, k, v, g = spread(*tiles_of(x_ref, (n,)))
        lane = lanes_like(q)
        valid = t0 + lax.broadcasted_iota(jnp.int32, q.shape, 0) < length
        q = jnp.where(lane < 96, q, jnp.where(lane == 96, 1.0, 0.0))
        k = jnp.where(lane < 96, k, jnp.where((lane == 96) & ~valid, MASKED, 0.0))
        v = jnp.where(lane < 96, v, jnp.where(lane < 98, 1.0, 0.0))
        g = jnp.where((lane < 96) & valid, g, 0.0)
        qx[pl.ds(t0, rows), :] = q.astype(BF16)
        kx[pl.ds(t0, rows), :] = k.astype(BF16)
        vx[pl.ds(t0, rows), :] = v.astype(BF16)
        cot[pl.ds(t0 + FRONT, rows), :] = g
        return 0

    lax.fori_loop(0, blocks, load, 0)

    def turn(n, _):
        t0 = pl.multiple_of(n * 256, 256)
        kt[:, pl.ds(t0, 256)] = kx[pl.ds(t0, 256), :].astype(F32).T.astype(BF16)
        vt[:, pl.ds(t0, 256)] = vx[pl.ds(t0, 256), :].astype(F32).T.astype(BF16)
        return 0

    lax.fori_loop(0, frames // 256, turn, 0)

    def valid_rows(t0, count):
        return t0 + lax.broadcasted_iota(jnp.int32, (count, LANES), 0) < length

    def conv_cot(t0, count):
        total = cot[pl.ds(t0 + FRONT, count), :]
        for j in range(TAPS):
            total = total + taps_ref[j : j + 1, :] * cot[pl.ds(t0 + FRONT + HALF - j, count), :]
        cgr[pl.ds(t0, count), :] = jnp.where(valid_rows(t0, count), total, 0.0)

    def conv_ctx(t0, count):
        total = ctx[pl.ds(t0 + FRONT, count), :]
        g = cot[pl.ds(t0 + FRONT, count), :]
        for j in range(TAPS):
            shifted = ctx[pl.ds(t0 + FRONT + j - HALF, count), :]
            total = total + taps_ref[j : j + 1, :] * shifted
            acc[j] += jnp.sum((g * shifted).reshape(count // 8, 8, LANES), axis=0)
        bo[pl.ds(t0 + 16, count), :] = jnp.where(valid_rows(t0, count), total, 0.0)

    def block(i, _):
        q0 = pl.multiple_of(i * QUERY_BLOCK, QUERY_BLOCK)
        qb = qx[pl.ds(q0, QUERY_BLOCK), :]

        def scores(n, top):
            k0 = pl.multiple_of(n * KEY_CHUNK, KEY_CHUNK)
            s = dot(kx[pl.ds(k0, KEY_CHUNK), :], qb, NT)
            s_buf[pl.ds(k0, KEY_CHUNK), :] = s
            conv_cot(pl.multiple_of(q0 + n * step, 8), step)
            return jnp.maximum(top, jnp.max(s.reshape(KEY_CHUNK // 8, 8, QUERY_BLOCK), axis=0))

        top = lax.fori_loop(0, chunks, scores, jnp.full((8, QUERY_BLOCK), -3e38, F32))
        top = jnp.max(top, axis=0, keepdims=True) * c
        ot[...] = jnp.zeros_like(ot)
        dqt[...] = jnp.zeros_like(dqt)

        def expo(n, _):
            k0 = pl.multiple_of(n * KEY_CHUNK, KEY_CHUNK)
            e = jnp.exp2(s_buf[pl.ds(k0, KEY_CHUNK), :] * c - top).astype(BF16)
            e_buf[pl.ds(k0, KEY_CHUNK), :] = e
            ot[...] += dot(vt[:, pl.ds(k0, KEY_CHUNK)], e)
            return 0

        lax.fori_loop(0, chunks, expo, 0)
        o = ot[...]
        inv = 1.0 / o[96:97, :]
        row = lax.broadcasted_iota(jnp.int32, o.shape, 0)
        context = (o * inv).T.astype(BF16).astype(F32)
        ctx[pl.ds(q0 + FRONT, QUERY_BLOCK), :] = jnp.where(valid_rows(q0, QUERY_BLOCK), context, 0.0)
        grad = cgr[pl.ds(q0, QUERY_BLOCK), :].astype(BF16).astype(F32)
        gt = (grad.T * inv).astype(BF16).astype(F32)
        delta = -jnp.sum(gt * o, axis=0, keepdims=True) * inv
        high = delta.astype(BF16).astype(F32)
        gx = jnp.where(row == 96, high, jnp.where(row == 97, delta - high, gt)).astype(BF16)
        gb = gt.T.astype(BF16)

        def back(n, _):
            k0 = pl.multiple_of(n * KEY_CHUNK, KEY_CHUNK)
            e = e_buf[pl.ds(k0, KEY_CHUNK), :]
            ds = (e.astype(F32) * dot(vx[pl.ds(k0, KEY_CHUNK), :], gx)).astype(BF16)
            dqt[...] += dot(kt[:, pl.ds(k0, KEY_CHUNK)], ds)
            dk[pl.ds(k0, KEY_CHUNK), :] += dot(ds, qb)
            dv[pl.ds(k0, KEY_CHUNK), :] += dot(e, gb)
            conv_ctx(pl.multiple_of(q0 + n * step - 16, 8), step)
            return 0

        lax.fori_loop(0, chunks, back, 0)
        dq[pl.ds(q0, QUERY_BLOCK), :] = dqt[...].T * scaling
        return 0

    lax.fori_loop(0, frames // QUERY_BLOCK, block, 0)
    conv_ctx(frames - 16, 16)
    for j in range(TAPS):
        grad_ref[j : j + 1, :] = jnp.sum(acc[j], axis=0, keepdims=True)
    grad_ref[TAPS:, :] = jnp.zeros((grad_ref.shape[0] - TAPS, LANES), F32)

    def store(n, _):
        t0 = pl.multiple_of(n * rows, rows)
        at = pl.ds(t0, rows)
        tiles = squeeze(bo[pl.ds(t0 + 16, rows), :], dq[at, :], dk[at, :] * scaling, dv[at, :])
        for i, tile in enumerate(tiles):
            out_ref[n, :, LANES * i : LANES * (i + 1)] = tile.astype(BF16)
        return 0

    lax.fori_loop(0, blocks, store, 0)


def core(lengths, x, taps):
    blocks, rows, group = x.shape
    frames = blocks * rows
    vmem = pl.BlockSpec(memory_space=pltpu.VMEM)
    half = lambda *shape: pltpu.VMEM(shape, BF16)
    full = lambda *shape: pltpu.VMEM(shape, F32)
    return pl.pallas_call(
        core_kernel,
        in_specs=[pl.BlockSpec(memory_space=pltpu.SMEM), vmem, vmem],
        out_specs=[vmem, vmem],
        out_shape=[
            jax.ShapeDtypeStruct(x.shape, BF16),
            jax.ShapeDtypeStruct((32, LANES), F32),
        ],
        scratch_shapes=[
            half(frames, LANES), half(frames, LANES), half(frames, LANES),
            half(LANES, frames), half(LANES, frames),
            full(frames, QUERY_BLOCK), half(frames, QUERY_BLOCK),
            full(frames + 2 * FRONT, LANES), full(frames + 2 * FRONT, LANES),
            full(frames, LANES), full(frames + 16, LANES),
            full(frames, LANES), full(frames, LANES), full(frames, LANES),
            full(LANES, QUERY_BLOCK), full(LANES, QUERY_BLOCK),
            full(TAPS, 8, LANES),
        ],
        compiler_params=pltpu.CompilerParams(vmem_limit_bytes=52 * 2**20),
        name="core",
    )(lengths, x, taps)


def exchange(x, axis):
    return lax.all_to_all(x, axis, split_axis=0, concat_axis=0, tiled=True)


def on_device(queries, keys_in, values_in, lengths, kernel, cotangent):
    groups, parts = lax.axis_size("seq"), lax.axis_size("dp")
    x = exchange(pack((queries[0], keys_in[0], values_in[0], cotangent[0])), "seq")
    mine = lax.dynamic_slice_in_dim(kernel, lax.axis_index("seq") * HEAD_DIM, HEAD_DIM, axis=1)
    taps = jnp.pad(mine, ((0, 1), (0, LANES - HEAD_DIM)))
    packed, grad = core(lengths, x, taps)
    grad = exchange(jnp.broadcast_to(grad[None], (parts,) + grad.shape), "dp").sum(axis=0)
    block_out, query_grad, key_grad, value_grad = unpack(exchange(packed, "seq"))
    grads = exchange(jnp.broadcast_to(grad[None], (groups,) + grad.shape), "seq")
    kernel_grad = grads[:, :TAPS, :HEAD_DIM].transpose(1, 0, 2).reshape(kernel.shape)
    return (block_out[None], query_grad[None], key_grad[None], value_grad[None], kernel_grad)


def solution(mesh):
    frames = P("dp", "seq", None)
    return jax.shard_map(
        on_device,
        mesh=mesh,
        in_specs=(frames, frames, frames, P("dp"), P(), frames),
        out_specs=(frames, frames, frames, frames, P()),
        check_vma=False,
    )
```
